32 devices in a mesh: groups: 2 (over x), slab: 16 (over z, y, core).
Axes of the slice: x: 2, y: 2, z: 4, core: 2. Of those that a mesh axis runs over, the one named last changes fastest.
Arguments:
- slowness: float32 [64, 64, 128], P('slab', 'groups'), parts along dimension 1, may hold values from 0.5 to 2
- absorbing: int32 [64, 64, 128], P('slab', 'groups'), parts along dimension 1, may hold values 0 or 1
- src_cell: int32 [16], P('groups'), parts along dimension 0, may hold values from 0 to 262143
- src_amp: float32 [2, 16], P(None, 'groups'), parts along dimension 1, may hold values from -8 to 8
- rec_slab: int32 [16, 8192, 1], P('groups', 'slab'), parts along dimension 0, may hold values from 0 to 15; in each aligned block of 512 rows (0 to 511, 512 to 1023, ..., all dimensions but the last counted through in order) at most 96 rows name the same one
- rec_local: int32 [16, 8192], P('groups', 'slab'), parts along dimension 0, may hold values from 0 to 16383
- rec_data: float32 [2, 16, 8192], P(None, 'groups', 'slab'), parts along dimension 1, may hold values from -6 to 6
Outputs:
- wavefield: float32 [2, 16, 64, 32, 128], P(None, 'groups', 'slab'), parts along dimension 1
- updated: float32 [64, 64, 128], P('slab', 'groups'), parts along dimension 1
The draws below stay inside these ranges and needn't reach their ends.
There are 2 independent parts, one for each index of `groups`. The reference program is written for one: setup_inputs(seed, part) draws one part's arguments, and reference() takes and returns one part's arrays. A program takes and returns all parts, laid end to end along the dimension named above; each array names one. Nothing has to cross between parts.
Inputs may be any that keep to these rules, and one draw needn't show every extreme that they name: `rec_slab`: for each shot, among the 512 receivers of one aligned block of the receiver list, at most 96 lie in one slab; some block holds exactly 96 in some slab.
All inputs are finite; a program needn't handle non-finite values. No bound on the sum of `absorbing` on one device may be relied on, other than what follows from the above.
Results may differ from the reference program's by a relative error of at most 0.0001.
Values sent between devices are 32-bit elements; how exact they have to be, the bound alone decides.
A program may use at most 192 MiB of HBM per device.

```python
import math
import jax
import jax.numpy as jnp
import numpy as np

NX = 128
NY = 32
CZ = 4
SHOTS = 8
RDEV = 512
ITERS = 2
NZ = 64
NREC = 8192
CAP = 96
N_SLAB = 16


def touch_ends(entries, rng, smallest, largest):
    place = [jax.random.randint(jax.random.fold_in(rng, axis), (), 0, length) for axis, length in enumerate(entries.shape)]
    longest = entries.shape.index(max(entries.shape))
    next_to = place[:longest] + [(place[longest] + 1) % entries.shape[longest]] + place[longest + 1:]
    return entries.at[tuple(place)].set(smallest).at[tuple(next_to)].set(largest)


def levels(key, dims, shards, smallest, largest):
    factor_of, own = 1.0, jax.random.fold_in(key, 6)
    for axis_at, shards_of in shards:
        steps = jnp.exp(jax.random.uniform(jax.random.fold_in(own, axis_at), (shards_of,), jnp.float32, smallest / len(shards), largest / len(shards)))
        factor_of = factor_of * jnp.repeat(steps, dims[axis_at] // shards_of).reshape([-1 if axis == axis_at else 1 for axis in range(len(dims))])
    return factor_of


def deal_out(stream_key, own, number, rows, amount, top, bound, skew):
    order = jax.random.permutation(stream_key, amount)
    packed, common = load_shares(amount, rows * top, bound, skew, True), load_shares(amount, rows * top, bound, skew, False)
    places = jnp.arange(amount)

    def named(sizes, offset_by):
        used = int((sizes > 0).sum())
        fixed = max(1, used // 4)
        moved = fixed + (places - fixed + offset_by * (used - fixed)) % max(1, amount - fixed)
        return jnp.zeros((amount,), jnp.int32).at[order[jnp.where(places < fixed, places, moved)]].set(jnp.asarray(sizes, jnp.int32))

    sizes = jnp.where(number % 4 == 0, named(packed, number // 4), named(common, number - number // 4 - 1))
    mixed = jax.random.permutation(jax.random.fold_in(own, 3), amount)
    source_of, receiver = mixed[0:amount // 2 * 2:2], mixed[1:amount // 2 * 2:2]
    room = jnp.minimum(sizes[source_of] - 1, bound - sizes[receiver]) // 2
    room = jnp.where((source_of == order[0]) | (receiver == order[0]) | (sizes[receiver] == 0), 0, jnp.maximum(room, 0))
    moved = jax.random.randint(jax.random.fold_in(own, 4), (amount // 2,), 0, 1 << 20) % (room + 1)
    sizes = sizes.at[source_of].add(-moved).at[receiver].add(moved)
    members = jnp.searchsorted(jnp.cumsum(sizes), jnp.arange(rows * top), side="right").astype(jnp.int32)
    listing = members.reshape(top, rows).T
    listing = listing[jax.random.permutation(jax.random.fold_in(own, 1), rows)]
    offset_by = jax.random.randint(jax.random.fold_in(own, 2), (rows, 1), 0, top)
    return jnp.take_along_axis(listing, (jnp.arange(top)[None, :] + offset_by) % top, axis=1)


def load_shares(amount, total, limit, slope, full):
    weights = [(1 << 20) // math.isqrt(standing ** slope) + 1 for standing in range(1, amount + 1)]
    largest = limit if full else min(limit, max(-(-total // amount), total * weights[0] // sum(weights)))
    least = 1 if total - largest >= amount - 1 else 0
    holding, surplus = [largest] + [least] * (amount - 1), total - largest - least * (amount - 1)
    while surplus > 0:
        free = [i for i in range(1, amount) if holding[i] < largest] or [i for i in range(1, amount) if holding[i] < limit]
        mass, left = sum([weights[i] for i in free]), surplus
        for i in free:
            extra = min(limit - holding[i], max(1, left * weights[i] // mass), surplus)
            holding[i] = holding[i] + extra
            surplus = surplus - extra
    return np.array(holding)


def centred(key, extent, width, limit, cuts=(), kind=jnp.bfloat16):
    level = levels(key, extent, cuts, -0.22, 0.18) if cuts else 1.0
    values = jax.random.normal(key, extent, jnp.float32) * width * level
    return jnp.minimum(jnp.maximum(values, -limit), limit).astype(kind)


def setup_inputs(seed: int = 0, part: int = 0) -> dict:
    arg_keys = jax.random.split(jax.random.key(seed), 8)
    own_keys = jax.random.split(jax.random.fold_in(arg_keys[7], part), 8)
    slowness = jnp.clip(jnp.exp(math.log(2.0) - 1.3862944 * jax.random.uniform(own_keys[0], (NZ, NY, NX), jnp.float32) ** levels(own_keys[0], (NZ, NY, NX), ((0, 16),), -0.2, 0.2)), 0.5, 2.0)
    absorbing = touch_ends((jax.random.randint(own_keys[1], (NZ, NY, NX), 0, 3) < 1).astype(jnp.int32), jax.random.fold_in(own_keys[1], 1), 0, 1)
    src_cell = touch_ends(jax.random.randint(own_keys[2], (SHOTS,), 0, NZ * NY * NX), jax.random.fold_in(own_keys[2], 1), 0, (NZ * NY * NX) - 1).astype(jnp.int32)
    src_amp = centred(own_keys[3], (2, SHOTS), 2.0, 8.0, (), jnp.float32)
    rec_slab_keys = jax.random.split(jax.random.fold_in(own_keys[4], 1), SHOTS * NREC // RDEV)
    rec_slab_turns = jax.random.permutation(jax.random.fold_in(own_keys[4], 3), SHOTS * NREC // RDEV)
    rec_slab = jax.vmap(lambda own, number: deal_out(jax.random.fold_in(own_keys[4], 2), own, number, RDEV, N_SLAB, 1, CAP, 2))(rec_slab_keys, rec_slab_turns).reshape((SHOTS, NREC, 1))
    rec_local = touch_ends(jax.random.randint(own_keys[5], (SHOTS, NREC), 0, CZ * NY * NX), jax.random.fold_in(own_keys[5], 1), 0, (CZ * NY * NX) - 1).astype(jnp.int32)
    rec_data = centred(own_keys[6], (2, SHOTS, NREC), 1.0, 6.0, ((2, 16),), jnp.float32)
    return dict(slowness=slowness, absorbing=absorbing, src_cell=src_cell, src_amp=src_amp, rec_slab=rec_slab, rec_local=rec_local, rec_data=rec_data)


K_SQ = 0.8
DAMPING = 0.6
PENALTY = 4.0
REGULAR = 0.5


def laplace(field):
    padded = jnp.pad(field, ((0, 0), (0, 0), (1, 1), (1, 1), (1, 1)))
    beside = padded[:, :, 2:, 1:-1, 1:-1] + padded[:, :, :-2, 1:-1, 1:-1]
    beside = beside + padded[:, :, 1:-1, 2:, 1:-1] + padded[:, :, 1:-1, :-2, 1:-1]
    beside = beside + padded[:, :, 1:-1, 1:-1, 2:] + padded[:, :, 1:-1, 1:-1, :-2]
    return 6.0 * field - beside


def helmholtz(field, coeff, lossy, sign):
    lap = laplace(field)
    real_part = lap[0] - coeff * field[0] + sign * lossy * field[1]
    imag_part = lap[1] - coeff * field[1] - sign * lossy * field[0]
    return jnp.stack([real_part, imag_part])


def inner(left, right):
    return jnp.sum(left * right, axis=(0, 2, 3, 4))


def reference(slowness, absorbing, src_cell, src_amp, rec_slab, rec_local, rec_data):
    total = NZ * NY * NX
    mask_f = absorbing.astype(jnp.float32)
    coeff = K_SQ * slowness
    lossy = DAMPING * coeff * mask_f
    flat = rec_slab[:, :, 0] * (CZ * NY * NX) + rec_local

    def per_shot(idx, values):
        return jax.ops.segment_sum(values, idx, num_segments=total)

    weight = jax.vmap(per_shot)(flat, jnp.ones((SHOTS, NREC), jnp.float32)).reshape(SHOTS, NZ, NY, NX)
    pdata = jnp.stack([jax.vmap(per_shot)(flat, rec_data[0]), jax.vmap(per_shot)(flat, rec_data[1])])
    pdata = pdata.reshape(2, SHOTS, NZ, NY, NX)
    cells = jnp.arange(total, dtype=jnp.int32)
    hit = (cells[None, :] == src_cell[:, None]).astype(jnp.float32)
    source = (src_amp[:, :, None] * hit[None]).reshape(2, SHOTS, NZ, NY, NX)

    def normal(vec):
        image = helmholtz(vec, coeff, lossy, 1.0)
        return helmholtz(image, coeff, lossy, -1.0) + PENALTY * weight[None] * vec

    rhs = helmholtz(source, coeff, lossy, -1.0) + PENALTY * pdata
    wavefield = jnp.zeros_like(rhs)
    residual = rhs
    direction = rhs
    norm_now = inner(residual, residual)
    for step in range(ITERS):
        image = normal(direction)
        alpha = (norm_now / inner(direction, image))[None, :, None, None, None]
        wavefield = wavefield + alpha * direction
        residual = residual - alpha * image
        norm_next = inner(residual, residual)
        beta = (norm_next / norm_now)[None, :, None, None, None]
        direction = residual + beta * direction
        norm_now = norm_next
    misfit = helmholtz(wavefield, coeff, lossy, 1.0) - source
    scaled = DAMPING * mask_f
    grad_r = -K_SQ * (wavefield[0] - scaled * wavefield[1])
    grad_i = -K_SQ * (wavefield[1] + scaled * wavefield[0])
    numer = jnp.sum(grad_r * misfit[0] + grad_i * misfit[1], axis=0)
    denom = jnp.sum(grad_r * grad_r + grad_i * grad_i, axis=0)
    updated = slowness - numer / (denom + REGULAR)
    return wavefield, updated
```

```python
import functools

import jax
import jax.numpy as jnp
from jax import lax
from jax.experimental import pallas as pl
from jax.experimental.pallas import tpu as pltpu
from jax.sharding import PartitionSpec as P

K_SQ = 0.8
DAMPING = 0.6
PENALTY = 4.0
REGULAR = 0.5

LANES = 128
GROUP = 4
KINDS = 3
F32 = jnp.float32
BF16 = jnp.bfloat16
MESH = pl.DeviceIdType.MESH
NT = (((1,), (1,)), ((), ()))


def spread(row, rows):
    tile = jnp.broadcast_to(row, (16, row.shape[1])).astype(BF16)
    return jnp.concatenate([tile] * (rows // 16), axis=0)


def ramp(shape):
    return lax.broadcasted_iota(jnp.int32, shape, 0).astype(F32).astype(BF16)


def split(values):
    high = values.astype(BF16).astype(F32)
    return high, (values - high).astype(BF16).astype(F32)


def kernel(
    count, depth, height, slots,
    slow_ref, absorb_ref, cell_ref, amp_ref, own_ref, loc_ref, dat_ref,
    wave_ref, upd_ref,
    feats, ranks, send, recv, parts, weight, field, image, normal, rest, rest_image,
    halo, stat_a, all_a, stat_b, all_b, scal,
    route_s, route_r, sum_s, sum_r, halo_s, halo_r,
):
    me = lax.axis_index("slab")
    shots, block = own_ref.shape
    cells, width = slow_ref.shape
    dot = functools.partial(lax.dot_general, preferred_element_type=F32)

    def others(body):
        lax.fori_loop(1, count, lambda k, c: (body(k), c)[1], 0)

    def each_shot(body):
        lax.fori_loop(0, shots, lambda s, c: (body(s), c)[1], 0)

    barrier = pltpu.get_barrier_semaphore()

    def greet(k):
        pl.semaphore_signal(
            barrier, inc=1, device_id={"slab": lax.rem(me + k, count)}, device_id_type=MESH
        )

    others(greet)

    own, loc = own_ref[...], loc_ref[...]
    column = loc & (width - 1)
    real_hi, real_lo = split(dat_ref[0])
    imag_hi, imag_lo = split(dat_ref[1])
    zero = jnp.zeros((shots, block), F32)
    rows = [(loc - column).astype(F32), real_hi, imag_hi] + [zero] * 5
    rows += [(column + 1).astype(F32), real_lo, imag_lo] + [zero] * 5
    for at, row in enumerate(rows):
        feats[:, at, :] = row
    named = jnp.concatenate(
        [jnp.where(own == slab, 1.0, 0.0) for slab in range(count)], axis=0
    )
    first = lax.broadcasted_iota(jnp.int32, (block, block), 0)
    later = lax.broadcasted_iota(jnp.int32, (block, block), 1)
    before = jnp.where(first < later, 1.0, 0.0).astype(BF16)
    ahead = dot(named.astype(BF16), before, (((1,), (0,)), ((), ())))
    ranks[...] = jnp.where(named > 0.0, ahead, -1.0)

    slot = ramp((slots, block))
    one = jnp.ones((), BF16)
    nought = jnp.zeros((), BF16)

    def compact(s):
        values = feats[s].astype(BF16)
        for base in range(0, count, GROUP):
            picks = jnp.concatenate(
                [
                    jnp.where(
                        slot == spread(ranks[pl.ds(slab * shots + s, 1), :], slots), one, nought
                    )
                    for slab in range(base, base + GROUP)
                ],
                axis=0,
            )
            out = dot(values, picks, NT)
            out = out[:8] + out[8:]
            for i in range(GROUP):
                for kind in range(KINDS):
                    send[base + i, kind, pl.ds(s, 1), :] = out[
                        kind : kind + 1, i * slots : (i + 1) * slots
                    ]

    each_shot(compact)
    pl.semaphore_wait(barrier, count - 1)

    def routed(k):
        target = lax.rem(me + k, count)
        return pltpu.make_async_remote_copy(
            src_ref=send.at[target], dst_ref=recv.at[me],
            send_sem=route_s.at[k], recv_sem=route_r.at[k],
            device_id={"slab": target}, device_id_type=MESH,
        )

    def landed(k):
        source = lax.rem(me + count - k, count)
        return pltpu.make_async_remote_copy(
            src_ref=send.at[source], dst_ref=recv.at[source],
            send_sem=route_s.at[k], recv_sem=route_r.at[k],
            device_id={"slab": source}, device_id_type=MESH,
        )

    others(lambda k: routed(k).start())
    recv[me] = send[me]

    coeff = K_SQ * slow_ref[...]
    mask = absorb_ref[...].astype(F32)
    lossy = DAMPING * coeff * mask
    row_of = lax.broadcasted_iota(jnp.int32, (cells, width), 0)
    x_of = lax.broadcasted_iota(jnp.int32, (cells, width), 1)
    z_of = row_of // height + me * depth
    y_of = row_of % height
    at_top, at_bottom = y_of == 0, y_of == height - 1
    at_left, at_right = x_of == 0, x_of == width - 1

    def far(s):
        cell = cell_ref[s]
        plane = cell // (height * width)
        line = (cell // width) % height
        place = cell % width
        return jnp.abs(z_of - plane) + jnp.abs(y_of - line) + jnp.abs(x_of - place)

    def laplace(centre, low, high):
        beside = jnp.concatenate([centre[height:], high], axis=0)
        beside = beside + jnp.concatenate([low, centre[:-height]], axis=0)
        beside = beside + jnp.where(at_top, 0.0, pltpu.roll(centre, 1, 0))
        beside = beside + jnp.where(at_bottom, 0.0, pltpu.roll(centre, cells - 1, 0))
        beside = beside + jnp.where(at_left, 0.0, pltpu.roll(centre, 1, 1))
        beside = beside + jnp.where(at_right, 0.0, pltpu.roll(centre, width - 1, 1))
        return 6.0 * centre - beside

    def helmholtz(real, imag, low, high, sign):
        out_r = laplace(real, low[0], high[0]) - coeff * real + sign * lossy * imag
        out_i = laplace(imag, low[1], high[1]) - coeff * imag - sign * lossy * real
        return out_r, out_i

    for step in range(3):
        @pl.when(me == 0)
        def _(step=step):
            halo[step, 0] = jnp.zeros(halo.shape[2:], F32)

        @pl.when(me == count - 1)
        def _(step=step):
            halo[step, 1] = jnp.zeros(halo.shape[2:], F32)

    def edge(step, ref, s, side):
        target = me + 1 if side == 0 else me - 1
        at = cells - height if side == 0 else 0
        return pltpu.make_async_remote_copy(
            src_ref=ref.at[s, :, pl.ds(at, height), :], dst_ref=halo.at[step, side, s],
            send_sem=halo_s.at[step, side, s], recv_sem=halo_r.at[step, side, s],
            device_id={"slab": target}, device_id_type=MESH,
        )

    has = [me > 0, me < count - 1]

    def send_edges(step, ref, s):
        pl.when(has[1])(lambda: edge(step, ref, s, 0).start())
        pl.when(has[0])(lambda: edge(step, ref, s, 1).start())

    def wait_edges(step, ref, s):
        pl.when(has[0])(lambda: edge(step, ref, s, 0).wait_recv())
        pl.when(has[1])(lambda: edge(step, ref, s, 1).wait_recv())

    def sent_edges(step, ref, s):
        pl.when(has[1])(lambda: edge(step, ref, s, 0).wait_send())
        pl.when(has[0])(lambda: edge(step, ref, s, 1).wait_send())

    def along(values):
        return jnp.sum(values, axis=0, keepdims=True)

    def shared(which, ref, gathered, k):
        target = lax.rem(me + k, count)
        return pltpu.make_async_remote_copy(
            src_ref=ref, dst_ref=gathered.at[me],
            send_sem=sum_s.at[which, k], recv_sem=sum_r.at[which, k],
            device_id={"slab": target}, device_id_type=MESH,
        )

    def heard(which, ref, gathered, k):
        source = lax.rem(me + count - k, count)
        return pltpu.make_async_remote_copy(
            src_ref=ref, dst_ref=gathered.at[source],
            send_sem=sum_s.at[which, k], recv_sem=sum_r.at[which, k],
            device_id={"slab": source}, device_id_type=MESH,
        )

    def totals(gathered):
        return jnp.sum(jnp.sum(gathered[...], axis=0), axis=-1, keepdims=True)

    others(lambda k: landed(k).wait_recv())
    place = recv[:, 0].astype(jnp.int32) - 1
    parts[0] = (place >> (width.bit_length() - 1)).astype(F32)
    parts[1] = (place & (width - 1)).astype(F32)
    parts[2], parts[3] = split(recv[:, 1])
    parts[4], parts[5] = split(recv[:, 2])

    wide = GROUP * slots
    cell_row = ramp((cells, wide))
    cell_col = ramp((width, wide))

    def gather(s):
        total = None
        for base in range(0, count, GROUP):
            def line(kind, length):
                row = jnp.concatenate(
                    [parts[kind, base + i, pl.ds(s, 1), :] for i in range(GROUP)], axis=1
                )
                return spread(row, length)

            left = jnp.where(cell_row == line(0, cells), one, nought)
            same = cell_col == line(1, width)
            right = jnp.concatenate(
                [jnp.where(same, one, nought)]
                + [jnp.where(same, line(kind, width), nought) for kind in range(2, 6)],
                axis=0,
            )
            piece = dot(left, right, NT)
            total = piece if total is None else total + piece
        weight[s] = PENALTY * total[:, :width]
        data_r = total[:, width : 2 * width] + total[:, 2 * width : 3 * width]
        data_i = total[:, 3 * width : 4 * width] + total[:, 4 * width :]
        away = far(s)
        here = jnp.where(away == 0, 1.0, 0.0)
        lap = jnp.where(away == 0, 6.0, jnp.where(away == 1, -1.0, 0.0)) - coeff * here
        turn = lossy * here
        amp_r, amp_i = amp_ref[0, s], amp_ref[1, s]
        field[s, 0] = amp_r * lap - amp_i * turn + PENALTY * data_r
        field[s, 1] = amp_i * lap + amp_r * turn + PENALTY * data_i
        send_edges(0, field, s)

    each_shot(gather)

    def apply_first(s):
        wait_edges(0, field, s)
        r, i = field[s, 0], field[s, 1]
        out_r, out_i = helmholtz(r, i, halo[0, 0, s], halo[0, 1, s], 1.0)
        image[s, 0] = out_r
        image[s, 1] = out_i
        send_edges(1, image, s)
        size = r * r + i * i
        stat_a[0, pl.ds(s, 1), :] = along(size)
        stat_a[1, pl.ds(s, 1), :] = along(out_r * out_r + out_i * out_i + weight[s] * size)

    each_shot(apply_first)
    others(lambda k: shared(0, stat_a, all_a, k).start())
    all_a[me] = stat_a[...]

    def apply_back(s):
        wait_edges(1, image, s)
        out_r, out_i = helmholtz(image[s, 0], image[s, 1], halo[1, 0, s], halo[1, 1, s], -1.0)
        normal[s, 0] = out_r + weight[s] * field[s, 0]
        normal[s, 1] = out_i + weight[s] * field[s, 1]
        send_edges(2, normal, s)

    each_shot(apply_back)
    others(lambda k: heard(0, stat_a, all_a, k).wait_recv())
    norm, curve = totals(all_a)
    alpha = norm / curve
    scal[0] = jnp.broadcast_to(alpha, (shots, LANES))

    def apply_second(s):
        wait_edges(2, normal, s)
        step = scal[0, pl.ds(s, 1), :]
        r = field[s, 0] - step * normal[s, 0]
        i = field[s, 1] - step * normal[s, 1]
        low = halo[0, 0, s] - step[None] * halo[2, 0, s]
        high = halo[0, 1, s] - step[None] * halo[2, 1, s]
        out_r, out_i = helmholtz(r, i, low, high, 1.0)
        rest[s, 0] = r
        rest[s, 1] = i
        rest_image[s, 0] = out_r
        rest_image[s, 1] = out_i
        size = r * r + i * i
        stat_b[0, pl.ds(s, 1), :] = along(size)
        stat_b[1, pl.ds(s, 1), :] = along(out_r * out_r + out_i * out_i + weight[s] * size)
        stat_b[2, pl.ds(s, 1), :] = along(
            out_r * image[s, 0] + out_i * image[s, 1]
            + weight[s] * (r * field[s, 0] + i * field[s, 1])
        )

    each_shot(apply_second)
    others(lambda k: shared(1, stat_b, all_b, k).start())
    all_b[me] = stat_b[...]
    others(lambda k: heard(1, stat_b, all_b, k).wait_recv())
    following, own_curve, cross = totals(all_b)
    beta = following / norm
    second = following / (own_curve + beta * (2.0 * cross + beta * curve))
    scal[1] = jnp.broadcast_to(second, (shots, LANES))
    scal[2] = jnp.broadcast_to(alpha + second * beta, (shots, LANES))

    scaled = DAMPING * mask

    def finish(s, carry):
        numer, denom = carry
        on_rest = scal[1, pl.ds(s, 1), :]
        on_field = scal[2, pl.ds(s, 1), :]
        here = jnp.where(far(s) == 0, 1.0, 0.0)
        u_r = on_field * field[s, 0] + on_rest * rest[s, 0]
        u_i = on_field * field[s, 1] + on_rest * rest[s, 1]
        wave_ref[0, s] = u_r
        wave_ref[1, s] = u_i
        mis_r = on_field * image[s, 0] + on_rest * rest_image[s, 0] - amp_ref[0, s] * here
        mis_i = on_field * image[s, 1] + on_rest * rest_image[s, 1] - amp_ref[1, s] * here
        grad_r = -K_SQ * (u_r - scaled * u_i)
        grad_i = -K_SQ * (u_i + scaled * u_r)
        return (
            numer + grad_r * mis_r + grad_i * mis_i,
            denom + grad_r * grad_r + grad_i * grad_i,
        )

    empty = jnp.zeros((cells, width), F32)
    numer, denom = lax.fori_loop(0, shots, finish, (empty, empty))
    upd_ref[...] = slow_ref[...] - numer / (denom + REGULAR)

    def drain(s):
        sent_edges(0, field, s)
        sent_edges(1, image, s)
        sent_edges(2, normal, s)

    each_shot(drain)

    def drain_small(k):
        routed(k).wait_send()
        shared(0, stat_a, all_a, k).wait_send()
        shared(1, stat_b, all_b, k).wait_send()

    others(drain_small)


def local(slowness, absorbing, src_cell, src_amp, rec_slab, rec_local, rec_data):
    count = lax.axis_size("slab")
    depth, height, width = slowness.shape
    cells = depth * height
    shots, block = rec_local.shape
    capacity = 3 * block // count
    slots = -(-capacity // LANES) * LANES
    vmem = pl.BlockSpec(memory_space=pltpu.VMEM)
    smem = pl.BlockSpec(memory_space=pltpu.SMEM)
    pair = pltpu.VMEM((shots, 2, cells, width), F32)
    dma = pltpu.SemaphoreType.DMA
    wavefield, updated = pl.pallas_call(
        functools.partial(kernel, count, depth, height, slots),
        out_shape=(
            jax.ShapeDtypeStruct((2, shots, cells, width), F32),
            jax.ShapeDtypeStruct((cells, width), F32),
        ),
        in_specs=[vmem, vmem, smem, smem, vmem, vmem, vmem],
        out_specs=(vmem, vmem),
        scratch_shapes=[
            pltpu.VMEM((shots, 16, block), F32),
            pltpu.VMEM((count * shots, block), F32),
            pltpu.VMEM((count, KINDS, shots, slots), F32),
            pltpu.VMEM((count, KINDS, shots, slots), F32),
            pltpu.VMEM((6, count, shots, slots), F32),
            pltpu.VMEM((shots, cells, width), F32),
            pair, pair, pair, pair, pair,
            pltpu.VMEM((3, 2, shots, 2, height, width), F32),
            pltpu.VMEM((2, shots, LANES), F32),
            pltpu.VMEM((count, 2, shots, LANES), F32),
            pltpu.VMEM((3, shots, LANES), F32),
            pltpu.VMEM((count, 3, shots, LANES), F32),
            pltpu.VMEM((3, shots, LANES), F32),
            dma((count,)), dma((count,)),
            dma((2, count)), dma((2, count)),
            dma((3, 2, shots)), dma((3, 2, shots)),
        ],
        compiler_params=pltpu.CompilerParams(
            collective_id=0, has_side_effects=True, vmem_limit_bytes=48 * 1024 * 1024
        ),
    )(
        slowness.reshape(cells, width),
        absorbing.reshape(cells, width),
        src_cell,
        src_amp,
        rec_slab.reshape(shots, block),
        rec_local,
        rec_data,
    )
    return (
        wavefield.reshape(2, shots, depth, height, width),
        updated.reshape(depth, height, width),
    )


def solution(mesh):
    return jax.shard_map(
        local,
        mesh=mesh,
        in_specs=(
            P("slab", "groups", None),
            P("slab", "groups", None),
            P("groups"),
            P(None, "groups"),
            P("groups", "slab", None),
            P("groups", "slab"),
            P(None, "groups", "slab"),
        ),
        out_specs=(P(None, "groups", "slab", None, None), P("slab", "groups", None)),
        check_vma=False,
    )
```

```python
import functools

import jax
import jax.numpy as jnp
from jax import lax
from jax.experimental import pallas as pl
from jax.experimental.pallas import tpu as pltpu
from jax.sharding import PartitionSpec as P

K_SQ = 0.8
DAMPING = 0.6
PENALTY = 4.0
REGULAR = 0.5

LANES = 128
GROUP = 4
KINDS = 3
F32 = jnp.float32
BF16 = jnp.bfloat16
MESH = pl.DeviceIdType.MESH
NT = (((1,), (1,)), ((), ()))


def spread(row, rows):
    tile = jnp.broadcast_to(row, (16, row.shape[1])).astype(BF16)
    return jnp.concatenate([tile] * (rows // 16), axis=0)


def ramp(shape):
    return lax.broadcasted_iota(jnp.int32, shape, 0).astype(F32).astype(BF16)


def split(values):
    high = values.astype(BF16).astype(F32)
    return high, (values - high).astype(BF16).astype(F32)


def kernel(
    count, depth, height, slots,
    slow_in, absorb_in, cell_ref, amp_ref, own_in, loc_in, dat_in,
    wave_out, upd_ref,
    wave_ref, slow_ref, absorb_ref, own_ref, loc_ref, dat_ref, sums,
    feats, ranks, send, recv, parts, weight, field, image, normal, rest, rest_image,
    halo, stat_a, note_a, all_a, stat_b, note_b, all_b, scal,
    load_s, store_s, route_s, route_r, sum_s, sum_r, halo_s, halo_r,
):
    me = lax.axis_index("slab")
    shots, block = loc_ref.shape
    cells, width = slow_ref.shape
    dot = functools.partial(lax.dot_general, preferred_element_type=F32)

    def others(body):
        lax.fori_loop(1, count, lambda k, c: (body(k), c)[1], 0)

    def each_shot(body):
        lax.fori_loop(0, shots, lambda s, c: (body(s), c)[1], 0)

    barrier = pltpu.get_barrier_semaphore()

    def greet(k):
        pl.semaphore_signal(
            barrier, inc=1, device_id={"slab": lax.rem(me + k, count)}, device_id_type=MESH
        )

    loads = [
        pltpu.make_async_copy(source, target, load_s.at[at])
        for at, (source, target) in enumerate(
            [(own_in, own_ref), (loc_in, loc_ref), (dat_in, dat_ref),
             (slow_in, slow_ref), (absorb_in, absorb_ref)]
        )
    ]
    for load in loads:
        load.start()
    others(greet)
    for load in loads[:3]:
        load.wait()

    own, loc = own_ref[:, 0, :], loc_ref[...]
    column = loc & (width - 1)
    real_hi, real_lo = split(dat_ref[0])
    imag_hi, imag_lo = split(dat_ref[1])
    zero = jnp.zeros((shots, block), F32)
    rows = [(loc - column).astype(F32), real_hi, imag_hi] + [zero] * 5
    rows += [(column + 1).astype(F32), real_lo, imag_lo] + [zero] * 5
    for at, row in enumerate(rows):
        feats[:, at, :] = row
    named = jnp.concatenate(
        [jnp.where(own == slab, 1.0, 0.0) for slab in range(count)], axis=0
    )
    first = lax.broadcasted_iota(jnp.int32, (block, block), 0)
    later = lax.broadcasted_iota(jnp.int32, (block, block), 1)
    before = jnp.where(first < later, 1.0, 0.0).astype(BF16)
    ahead = dot(named.astype(BF16), before, (((1,), (0,)), ((), ())))
    ranks[...] = jnp.where(named > 0.0, ahead, -1.0)

    slot = ramp((slots, block))
    one = jnp.ones((), BF16)
    nought = jnp.zeros((), BF16)

    def compact(s):
        values = feats[s].astype(BF16)
        for base in range(0, count, GROUP):
            picks = jnp.concatenate(
                [
                    jnp.where(
                        slot == spread(ranks[pl.ds(slab * shots + s, 1), :], slots), one, nought
                    )
                    for slab in range(base, base + GROUP)
                ],
                axis=0,
            )
            out = dot(values, picks, NT)
            out = out[:8] + out[8:]
            for i in range(GROUP):
                for kind in range(KINDS):
                    send[base + i, kind, pl.ds(s, 1), :] = out[
                        kind : kind + 1, i * slots : (i + 1) * slots
                    ]

    each_shot(compact)
    pl.semaphore_wait(barrier, count - 1)

    def routed(k):
        target = lax.rem(me + k, count)
        return pltpu.make_async_remote_copy(
            src_ref=send.at[target], dst_ref=recv.at[k],
            send_sem=route_s.at[k], recv_sem=route_r.at[k],
            device_id={"slab": target}, device_id_type=MESH,
        )

    others(lambda k: routed(k).start())
    recv[0] = send[me]
    for load in loads[3:]:
        load.wait()

    coeff = K_SQ * slow_ref[...]
    mask = absorb_ref[...].astype(F32)
    lossy = DAMPING * coeff * mask
    row_of = lax.broadcasted_iota(jnp.int32, (cells, width), 0)
    x_of = lax.broadcasted_iota(jnp.int32, (cells, width), 1)
    z_of = row_of // height + me * depth
    y_of = row_of % height
    at_top, at_bottom = y_of == 0, y_of == height - 1
    at_left, at_right = x_of == 0, x_of == width - 1

    def far(s):
        cell = cell_ref[s]
        plane = cell // (height * width)
        line = (cell // width) % height
        place = cell % width
        return jnp.abs(z_of - plane) + jnp.abs(y_of - line) + jnp.abs(x_of - place)

    def laplace(centre, low, high):
        beside = jnp.concatenate([centre[height:], high], axis=0)
        beside = beside + jnp.concatenate([low, centre[:-height]], axis=0)
        beside = beside + jnp.where(at_top, 0.0, pltpu.roll(centre, 1, 0))
        beside = beside + jnp.where(at_bottom, 0.0, pltpu.roll(centre, cells - 1, 0))
        beside = beside + jnp.where(at_left, 0.0, pltpu.roll(centre, 1, 1))
        beside = beside + jnp.where(at_right, 0.0, pltpu.roll(centre, width - 1, 1))
        return 6.0 * centre - beside

    def helmholtz(real, imag, low, high, sign):
        out_r = laplace(real, low[0], high[0]) - coeff * real + sign * lossy * imag
        out_i = laplace(imag, low[1], high[1]) - coeff * imag - sign * lossy * real
        return out_r, out_i

    for step in range(3):
        @pl.when(me == 0)
        def _(step=step):
            halo[step, 0] = jnp.zeros(halo.shape[2:], F32)

        @pl.when(me == count - 1)
        def _(step=step):
            halo[step, 1] = jnp.zeros(halo.shape[2:], F32)

    def edge(step, ref, s, side):
        target = me + 1 if side == 0 else me - 1
        at = cells - height if side == 0 else 0
        return pltpu.make_async_remote_copy(
            src_ref=ref.at[s, :, pl.ds(at, height), :], dst_ref=halo.at[step, side, s],
            send_sem=halo_s.at[step, side, s], recv_sem=halo_r.at[step, side, s],
            device_id={"slab": target}, device_id_type=MESH,
        )

    has = [me > 0, me < count - 1]

    def send_edges(step, ref, s):
        pl.when(has[1])(lambda: edge(step, ref, s, 0).start())
        pl.when(has[0])(lambda: edge(step, ref, s, 1).start())

    def wait_edges(step, ref, s):
        pl.when(has[0])(lambda: edge(step, ref, s, 0).wait_recv())
        pl.when(has[1])(lambda: edge(step, ref, s, 1).wait_recv())

    def sent_edges(step, ref, s):
        pl.when(has[1])(lambda: edge(step, ref, s, 0).wait_send())
        pl.when(has[0])(lambda: edge(step, ref, s, 1).wait_send())

    def along(values):
        return jnp.sum(values, axis=0, keepdims=True)

    def shared(which, note, gathered, k):
        return pltpu.make_async_remote_copy(
            src_ref=note, dst_ref=gathered.at[k],
            send_sem=sum_s.at[which, k], recv_sem=sum_r.at[which, k],
            device_id={"slab": lax.rem(me + k, count)}, device_id_type=MESH,
        )

    def diagonal(values):
        lane = lax.broadcasted_iota(jnp.int32, values.shape, 1)
        return jnp.where(lane == lax.broadcasted_iota(jnp.int32, values.shape, 0), values, 0.0)

    def share(which, stat, note, gathered):
        kinds = stat.shape[0] * shots
        own_sums = jnp.sum(stat[...].reshape(kinds, LANES), axis=1, keepdims=True)
        note[...] = along(diagonal(jnp.broadcast_to(own_sums, (kinds, LANES))))
        others(lambda k: shared(which, note, gathered, k).start())
        gathered[0] = note[...]

    def totals(which, stat, note, gathered):
        others(lambda k: shared(which, note, gathered, k).wait_recv())
        kinds = stat.shape[0] * shots
        line = jnp.sum(gathered[...], axis=0)
        column = jnp.sum(
            diagonal(jnp.broadcast_to(line, (kinds, LANES))), axis=1, keepdims=True
        )
        return [column[at : at + shots] for at in range(0, kinds, shots)]

    wide = GROUP * slots
    cell_row = ramp((cells, wide))
    cell_col = ramp((width, wide))

    def gather(base, s):
        def line(kind, length):
            row = jnp.concatenate(
                [parts[kind, base + i, pl.ds(s, 1), :] for i in range(GROUP)], axis=1
            )
            return spread(row, length)

        left = jnp.where(cell_row == line(0, cells), one, nought)
        same = cell_col == line(1, width)
        right = jnp.concatenate(
            [jnp.where(same, one, nought)]
            + [jnp.where(same, line(kind, width), nought) for kind in range(2, 6)],
            axis=0,
        )
        total = dot(left, right, NT)
        if base > 0:
            total = sums[s] + total
        if base + GROUP < count:
            sums[s] = total
            return
        weight[s] = PENALTY * total[:, :width]
        data_r = total[:, width : 2 * width] + total[:, 2 * width : 3 * width]
        data_i = total[:, 3 * width : 4 * width] + total[:, 4 * width :]
        away = far(s)
        here = jnp.where(away == 0, 1.0, 0.0)
        lap = jnp.where(away == 0, 6.0, jnp.where(away == 1, -1.0, 0.0)) - coeff * here
        turn = lossy * here
        amp_r, amp_i = amp_ref[0, s], amp_ref[1, s]
        field[s, 0] = amp_r * lap - amp_i * turn + PENALTY * data_r
        field[s, 1] = amp_i * lap + amp_r * turn + PENALTY * data_i
        send_edges(0, field, s)

    for base in range(0, count, GROUP):
        for k in range(max(base, 1), base + GROUP):
            routed(k).wait_recv()
        part = pl.ds(base, GROUP)
        place = recv[part, 0].astype(jnp.int32) - 1
        parts[0, part] = (place >> (width.bit_length() - 1)).astype(F32)
        parts[1, part] = (place & (width - 1)).astype(F32)
        parts[2, part], parts[3, part] = split(recv[part, 1])
        parts[4, part], parts[5, part] = split(recv[part, 2])
        each_shot(functools.partial(gather, base))

    def apply_first(s):
        wait_edges(0, field, s)
        r, i = field[s, 0], field[s, 1]
        out_r, out_i = helmholtz(r, i, halo[0, 0, s], halo[0, 1, s], 1.0)
        image[s, 0] = out_r
        image[s, 1] = out_i
        send_edges(1, image, s)
        size = r * r + i * i
        stat_a[0, pl.ds(s, 1), :] = along(size)
        stat_a[1, pl.ds(s, 1), :] = along(out_r * out_r + out_i * out_i + weight[s] * size)

    each_shot(apply_first)
    share(0, stat_a, note_a, all_a)

    def apply_back(s):
        wait_edges(1, image, s)
        out_r, out_i = helmholtz(image[s, 0], image[s, 1], halo[1, 0, s], halo[1, 1, s], -1.0)
        normal[s, 0] = out_r + weight[s] * field[s, 0]
        normal[s, 1] = out_i + weight[s] * field[s, 1]
        send_edges(2, normal, s)

    each_shot(apply_back)
    norm, curve = totals(0, stat_a, note_a, all_a)
    alpha = norm / curve
    scal[0] = jnp.broadcast_to(alpha, (shots, LANES))

    def apply_second(s):
        wait_edges(2, normal, s)
        step = scal[0, pl.ds(s, 1), :]
        r = field[s, 0] - step * normal[s, 0]
        i = field[s, 1] - step * normal[s, 1]
        low = halo[0, 0, s] - step[None] * halo[2, 0, s]
        high = halo[0, 1, s] - step[None] * halo[2, 1, s]
        out_r, out_i = helmholtz(r, i, low, high, 1.0)
        rest[s, 0] = r
        rest[s, 1] = i
        rest_image[s, 0] = out_r
        rest_image[s, 1] = out_i
        size = r * r + i * i
        stat_b[0, pl.ds(s, 1), :] = along(size)
        stat_b[1, pl.ds(s, 1), :] = along(out_r * out_r + out_i * out_i + weight[s] * size)
        stat_b[2, pl.ds(s, 1), :] = along(
            out_r * image[s, 0] + out_i * image[s, 1]
            + weight[s] * (r * field[s, 0] + i * field[s, 1])
        )

    each_shot(apply_second)
    share(1, stat_b, note_b, all_b)
    following, own_curve, cross = totals(1, stat_b, note_b, all_b)
    beta = following / norm
    second = following / (own_curve + beta * (2.0 * cross + beta * curve))
    scal[1] = jnp.broadcast_to(second, (shots, LANES))
    scal[2] = jnp.broadcast_to(alpha + second * beta, (shots, LANES))

    scaled = DAMPING * mask

    def store(s):
        return pltpu.make_async_copy(wave_ref.at[:, s], wave_out.at[:, s], store_s.at[s])

    def finish(s, carry):
        numer, denom = carry
        on_rest = scal[1, pl.ds(s, 1), :]
        on_field = scal[2, pl.ds(s, 1), :]
        here = jnp.where(far(s) == 0, 1.0, 0.0)
        u_r = on_field * field[s, 0] + on_rest * rest[s, 0]
        u_i = on_field * field[s, 1] + on_rest * rest[s, 1]
        wave_ref[0, s] = u_r
        wave_ref[1, s] = u_i
        store(s).start()
        mis_r = on_field * image[s, 0] + on_rest * rest_image[s, 0] - amp_ref[0, s] * here
        mis_i = on_field * image[s, 1] + on_rest * rest_image[s, 1] - amp_ref[1, s] * here
        grad_r = -K_SQ * (u_r - scaled * u_i)
        grad_i = -K_SQ * (u_i + scaled * u_r)
        return (
            numer + grad_r * mis_r + grad_i * mis_i,
            denom + grad_r * grad_r + grad_i * grad_i,
        )

    empty = jnp.zeros((cells, width), F32)
    numer, denom = lax.fori_loop(0, shots, finish, (empty, empty))
    upd_ref[...] = slow_ref[...] - numer / (denom + REGULAR)

    def drain(s):
        sent_edges(0, field, s)
        sent_edges(1, image, s)
        sent_edges(2, normal, s)
        store(s).wait()

    each_shot(drain)

    def drain_small(k):
        routed(k).wait_send()
        shared(0, note_a, all_a, k).wait_send()
        shared(1, note_b, all_b, k).wait_send()

    others(drain_small)


def local(slowness, absorbing, src_cell, src_amp, rec_slab, rec_local, rec_data):
    count = lax.axis_size("slab")
    depth, height, width = slowness.shape
    cells = depth * height
    shots, block = rec_local.shape
    capacity = 3 * block // count
    slots = -(-capacity // LANES) * LANES
    vmem = pl.BlockSpec(memory_space=pltpu.VMEM)
    hbm = pl.BlockSpec(memory_space=pltpu.HBM)
    smem = pl.BlockSpec(memory_space=pltpu.SMEM)
    pair = pltpu.VMEM((shots, 2, cells, width), F32)
    dma = pltpu.SemaphoreType.DMA
    wavefield, updated = pl.pallas_call(
        functools.partial(kernel, count, depth, height, slots),
        out_shape=(
            jax.ShapeDtypeStruct((2, shots, cells, width), F32),
            jax.ShapeDtypeStruct((cells, width), F32),
        ),
        in_specs=[hbm, hbm, smem, smem, hbm, hbm, hbm],
        out_specs=(hbm, vmem),
        scratch_shapes=[
            pltpu.VMEM((2, shots, cells, width), F32),
            pltpu.VMEM((cells, width), F32),
            pltpu.VMEM((cells, width), jnp.int32),
            pltpu.VMEM((shots, 1, block), jnp.int32),
            pltpu.VMEM((shots, block), jnp.int32),
            pltpu.VMEM((2, shots, block), F32),
            pltpu.VMEM((shots, cells, 5 * width), F32),
            pltpu.VMEM((shots, 16, block), F32),
            pltpu.VMEM((count * shots, block), F32),
            pltpu.VMEM((count, KINDS, shots, slots), F32),
            pltpu.VMEM((count, KINDS, shots, slots), F32),
            pltpu.VMEM((6, count, shots, slots), F32),
            pltpu.VMEM((shots, cells, width), F32),
            pair, pair, pair, pair, pair,
            pltpu.VMEM((3, 2, shots, 2, height, width), F32),
            pltpu.VMEM((2, shots, LANES), F32),
            pltpu.VMEM((1, LANES), F32),
            pltpu.VMEM((count, 1, LANES), F32),
            pltpu.VMEM((3, shots, LANES), F32),
            pltpu.VMEM((1, LANES), F32),
            pltpu.VMEM((count, 1, LANES), F32),
            pltpu.VMEM((3, shots, LANES), F32),
            dma((5,)), dma((shots,)), dma((count,)), dma((count,)),
            dma((2, count)), dma((2, count)),
            dma((3, 2, shots)), dma((3, 2, shots)),
        ],
        compiler_params=pltpu.CompilerParams(
            collective_id=0, has_side_effects=True, vmem_limit_bytes=60 * 1024 * 1024
        ),
    )(
        slowness.reshape(cells, width),
        absorbing.reshape(cells, width),
        src_cell,
        src_amp,
        rec_slab.reshape(shots, 1, block),
        rec_local,
        rec_data,
    )
    return (
        wavefield.reshape(2, shots, depth, height, width),
        updated.reshape(depth, height, width),
    )


def solution(mesh):
    return jax.shard_map(
        local,
        mesh=mesh,
        in_specs=(
            P("slab", "groups", None),
            P("slab", "groups", None),
            P("groups"),
            P(None, "groups"),
            P("groups", "slab", None),
            P("groups", "slab"),
            P(None, "groups", "slab"),
        ),
        out_specs=(P(None, "groups", "slab", None, None), P("slab", "groups", None)),
        check_vma=False,
    )
```

```python
import functools

import jax
import jax.numpy as jnp
from jax import lax
from jax.experimental import pallas as pl
from jax.experimental.pallas import tpu as pltpu
from jax.sharding import PartitionSpec as P

K_SQ = 0.8
DAMPING = 0.6
PENALTY = 4.0
REGULAR = 0.5

LANES = 128
SPAN = 768
KINDS = 3
F32 = jnp.float32
BF16 = jnp.bfloat16
MESH = pl.DeviceIdType.MESH
NT = (((1,), (1,)), ((), ()))


def spread(row, rows):
    tile = jnp.broadcast_to(row, (16, row.shape[1])).astype(BF16)
    return jnp.concatenate([tile] * (rows // 16), axis=0)


def ramp(shape):
    return lax.broadcasted_iota(jnp.int32, shape, 0).astype(F32).astype(BF16)


def split(values):
    high = values.astype(BF16).astype(F32)
    return high, (values - high).astype(BF16).astype(F32)


def kernel(
    count, depth, height, slots, capacity,
    slow_in, absorb_in, cell_ref, amp_ref, own_in, loc_in, dat_in,
    wave_out, upd_ref,
    wave_ref, slow_ref, absorb_ref, own_ref, loc_ref, dat_ref, sums,
    feats, ranks, send, recv, parts, weight, field, image, normal, rest, rest_image,
    halo, stat_a, note_a, all_a, stat_b, note_b, all_b, scal,
    load_s, store_s, route_s, route_r, sum_s, sum_r, halo_s, halo_r,
):
    me = lax.axis_index("slab")
    shots, block = loc_ref.shape
    cells, width = slow_ref.shape
    dot = functools.partial(lax.dot_general, preferred_element_type=F32)

    def others(body):
        lax.fori_loop(1, count, lambda k, c: (body(k), c)[1], 0)

    def each_shot(body):
        lax.fori_loop(0, shots, lambda s, c: (body(s), c)[1], 0)

    barrier = pltpu.get_barrier_semaphore()

    def greet(k):
        pl.semaphore_signal(
            barrier, inc=1, device_id={"slab": lax.rem(me + k, count)}, device_id_type=MESH
        )

    loads = [
        pltpu.make_async_copy(source, target, load_s.at[at])
        for at, (source, target) in enumerate(
            [(own_in, own_ref), (loc_in, loc_ref), (dat_in, dat_ref),
             (slow_in, slow_ref), (absorb_in, absorb_ref)]
        )
    ]
    for load in loads:
        load.start()
    others(greet)
    for load in loads[:3]:
        load.wait()

    own, loc = own_ref[:, 0, :], loc_ref[...]
    column = loc & (width - 1)
    real_hi, real_lo = split(dat_ref[0])
    imag_hi, imag_lo = split(dat_ref[1])
    rows = [(loc - column).astype(F32), (column + 1).astype(F32)]
    rows += [real_hi, real_lo, imag_hi, imag_lo]
    for at, row in enumerate(rows):
        feats[:, at, :] = row
    named = jnp.concatenate(
        [jnp.where(own == slab, 1.0, 0.0) for slab in range(count)], axis=0
    )
    first = lax.broadcasted_iota(jnp.int32, (block, block), 0)
    later = lax.broadcasted_iota(jnp.int32, (block, block), 1)
    before = jnp.where(first < later, 1.0, 0.0).astype(BF16)
    ahead = dot(named.astype(BF16), before, (((1,), (0,)), ((), ())))
    chosen = named * ahead
    rank = chosen[:shots]
    for slab in range(1, count):
        rank = rank + chosen[slab * shots : (slab + 1) * shots]
    ranks[...] = rank

    slot = ramp((slots, block))
    slab_of = ramp((count, block))
    one = jnp.ones((), BF16)
    nought = jnp.zeros((), BF16)

    def compact(s):
        right = jnp.where(slot == spread(ranks[pl.ds(s, 1), :], slots), one, nought)
        mine = slab_of == spread(own_ref[s].astype(F32), count)
        left = jnp.concatenate(
            [
                jnp.where(mine, spread(feats[s, at : at + 1, :], count), nought)
                for at in range(2 * KINDS)
            ],
            axis=0,
        )
        out = dot(left, right, NT)
        for kind in range(KINDS):
            at = 2 * kind * count
            value = out[at : at + count] + out[at + count : at + 2 * count]
            send[:, kind, pl.ds(s, 1), :] = value.reshape(count, 1, slots)

    each_shot(compact)
    pl.semaphore_wait(barrier, count - 1)

    def routed(k):
        target = lax.rem(me + k, count)
        return pltpu.make_async_remote_copy(
            src_ref=send.at[target], dst_ref=recv.at[k],
            send_sem=route_s.at[k], recv_sem=route_r.at[k],
            device_id={"slab": target}, device_id_type=MESH,
        )

    others(lambda k: routed(k).start())
    recv[0] = send[me]
    for load in loads[3:]:
        load.wait()

    coeff = K_SQ * slow_ref[...]
    mask = absorb_ref[...].astype(F32)
    lossy = DAMPING * coeff * mask
    row_of = lax.broadcasted_iota(jnp.int32, (cells, width), 0)
    x_of = lax.broadcasted_iota(jnp.int32, (cells, width), 1)
    z_of = row_of // height + me * depth
    y_of = row_of % height
    at_top, at_bottom = y_of == 0, y_of == height - 1
    at_left, at_right = x_of == 0, x_of == width - 1

    def far(s):
        cell = cell_ref[s]
        plane = cell // (height * width)
        line = (cell // width) % height
        place = cell % width
        return jnp.abs(z_of - plane) + jnp.abs(y_of - line) + jnp.abs(x_of - place)

    def laplace(centre, low, high):
        beside = jnp.concatenate([centre[height:], high], axis=0)
        beside = beside + jnp.concatenate([low, centre[:-height]], axis=0)
        beside = beside + jnp.where(at_top, 0.0, pltpu.roll(centre, 1, 0))
        beside = beside + jnp.where(at_bottom, 0.0, pltpu.roll(centre, cells - 1, 0))
        beside = beside + jnp.where(at_left, 0.0, pltpu.roll(centre, 1, 1))
        beside = beside + jnp.where(at_right, 0.0, pltpu.roll(centre, width - 1, 1))
        return 6.0 * centre - beside

    def helmholtz(real, imag, low, high, sign):
        out_r = laplace(real, low[0], high[0]) - coeff * real + sign * lossy * imag
        out_i = laplace(imag, low[1], high[1]) - coeff * imag - sign * lossy * real
        return out_r, out_i

    for step in range(3):
        @pl.when(me == 0)
        def _(step=step):
            halo[step, 0] = jnp.zeros(halo.shape[2:], F32)

        @pl.when(me == count - 1)
        def _(step=step):
            halo[step, 1] = jnp.zeros(halo.shape[2:], F32)

    def edge(step, ref, s, side):
        target = me + 1 if side == 0 else me - 1
        at = cells - height if side == 0 else 0
        return pltpu.make_async_remote_copy(
            src_ref=ref.at[s, :, pl.ds(at, height), :], dst_ref=halo.at[step, side, s],
            send_sem=halo_s.at[step, side, s], recv_sem=halo_r.at[step, side, s],
            device_id={"slab": target}, device_id_type=MESH,
        )

    has = [me > 0, me < count - 1]

    def send_edges(step, ref, s):
        pl.when(has[1])(lambda: edge(step, ref, s, 0).start())
        pl.when(has[0])(lambda: edge(step, ref, s, 1).start())

    def wait_edges(step, ref, s):
        pl.when(has[0])(lambda: edge(step, ref, s, 0).wait_recv())
        pl.when(has[1])(lambda: edge(step, ref, s, 1).wait_recv())

    def sent_edges(step, ref, s):
        pl.when(has[1])(lambda: edge(step, ref, s, 0).wait_send())
        pl.when(has[0])(lambda: edge(step, ref, s, 1).wait_send())

    def along(values):
        return jnp.sum(values, axis=0, keepdims=True)

    def shared(which, note, gathered, k):
        return pltpu.make_async_remote_copy(
            src_ref=note, dst_ref=gathered.at[k],
            send_sem=sum_s.at[which, k], recv_sem=sum_r.at[which, k],
            device_id={"slab": lax.rem(me + k, count)}, device_id_type=MESH,
        )

    def diagonal(values):
        lane = lax.broadcasted_iota(jnp.int32, values.shape, 1)
        return jnp.where(lane == lax.broadcasted_iota(jnp.int32, values.shape, 0), values, 0.0)

    def share(which, stat, note, gathered):
        kinds = stat.shape[0] * shots
        own_sums = jnp.sum(stat[...].reshape(kinds, LANES), axis=1, keepdims=True)
        note[...] = along(diagonal(jnp.broadcast_to(own_sums, (kinds, LANES))))
        others(lambda k: shared(which, note, gathered, k).start())
        gathered[0] = note[...]

    def totals(which, stat, note, gathered):
        others(lambda k: shared(which, note, gathered, k).wait_recv())
        kinds = stat.shape[0] * shots
        line = jnp.sum(gathered[...], axis=0)
        column = jnp.sum(
            diagonal(jnp.broadcast_to(line, (kinds, LANES))), axis=1, keepdims=True
        )
        return [column[at : at + shots] for at in range(0, kinds, shots)]

    group = min(count, SPAN // capacity)
    wide = group * capacity
    half = cells // 2
    cell_row = ramp((half, wide))
    cell_col = ramp((2 * width, wide))

    def gather(base, s):
        def line(kind, length):
            return spread(parts[base // group, kind, pl.ds(s, 1), :], length)

        right = jnp.where(cell_col == line(1, 2 * width), one, nought)
        same = cell_row == line(0, half)
        left = jnp.concatenate(
            [jnp.where(same, one, nought)]
            + [jnp.where(same, line(kind, half), nought) for kind in range(2, 6)],
            axis=0,
        )
        total = dot(left, right, NT)
        if base > 0:
            total = sums[s] + total
        if base + group < count:
            sums[s] = total
            return

        def field_of(at):
            piece = total[at * half : (at + 1) * half]
            return jnp.concatenate([piece[:, :width], piece[:, width:]], axis=0)

        weight[s] = PENALTY * field_of(0)
        data_r = field_of(1) + field_of(2)
        data_i = field_of(3) + field_of(4)
        away = far(s)
        here = jnp.where(away == 0, 1.0, 0.0)
        lap = jnp.where(away == 0, 6.0, jnp.where(away == 1, -1.0, 0.0)) - coeff * here
        turn = lossy * here
        amp_r, amp_i = amp_ref[0, s], amp_ref[1, s]
        field[s, 0] = amp_r * lap - amp_i * turn + PENALTY * data_r
        field[s, 1] = amp_i * lap + amp_r * turn + PENALTY * data_i
        send_edges(0, field, s)

    for base in range(0, count, group):
        for k in range(max(base, 1), base + group):
            routed(k).wait_recv()
        cell, real, imag = [
            jnp.concatenate(
                [recv[k, kind][:, :capacity] for k in range(base, base + group)], axis=1
            )
            for kind in range(KINDS)
        ]
        cell = cell.astype(jnp.int32) - 1
        line_of = cell >> (width.bit_length() - 1)
        place = (cell & (width - 1)) + jnp.where(line_of >= half, width, 0)
        at = base // group
        parts[at, 0] = (line_of & (half - 1)).astype(F32)
        parts[at, 1] = jnp.where(cell < 0, -1, place).astype(F32)
        parts[at, 2], parts[at, 3] = split(real)
        parts[at, 4], parts[at, 5] = split(imag)
        each_shot(functools.partial(gather, base))

    def apply_first(s):
        wait_edges(0, field, s)
        r, i = field[s, 0], field[s, 1]
        out_r, out_i = helmholtz(r, i, halo[0, 0, s], halo[0, 1, s], 1.0)
        image[s, 0] = out_r
        image[s, 1] = out_i
        send_edges(1, image, s)
        size = r * r + i * i
        stat_a[0, pl.ds(s, 1), :] = along(size)
        stat_a[1, pl.ds(s, 1), :] = along(out_r * out_r + out_i * out_i + weight[s] * size)

    each_shot(apply_first)
    share(0, stat_a, note_a, all_a)

    def apply_back(s):
        wait_edges(1, image, s)
        out_r, out_i = helmholtz(image[s, 0], image[s, 1], halo[1, 0, s], halo[1, 1, s], -1.0)
        normal[s, 0] = out_r + weight[s] * field[s, 0]
        normal[s, 1] = out_i + weight[s] * field[s, 1]
        send_edges(2, normal, s)

    each_shot(apply_back)
    norm, curve = totals(0, stat_a, note_a, all_a)
    alpha = norm / curve
    scal[0] = jnp.broadcast_to(alpha, (shots, LANES))

    def apply_second(s):
        wait_edges(2, normal, s)
        step = scal[0, pl.ds(s, 1), :]
        r = field[s, 0] - step * normal[s, 0]
        i = field[s, 1] - step * normal[s, 1]
        low = halo[0, 0, s] - step[None] * halo[2, 0, s]
        high = halo[0, 1, s] - step[None] * halo[2, 1, s]
        out_r, out_i = helmholtz(r, i, low, high, 1.0)
        rest[s, 0] = r
        rest[s, 1] = i
        rest_image[s, 0] = out_r
        rest_image[s, 1] = out_i
        size = r * r + i * i
        stat_b[0, pl.ds(s, 1), :] = along(size)
        stat_b[1, pl.ds(s, 1), :] = along(out_r * out_r + out_i * out_i + weight[s] * size)
        stat_b[2, pl.ds(s, 1), :] = along(
            out_r * image[s, 0] + out_i * image[s, 1]
            + weight[s] * (r * field[s, 0] + i * field[s, 1])
        )

    each_shot(apply_second)
    share(1, stat_b, note_b, all_b)
    following, own_curve, cross = totals(1, stat_b, note_b, all_b)
    beta = following / norm
    second = following / (own_curve + beta * (2.0 * cross + beta * curve))
    scal[1] = jnp.broadcast_to(second, (shots, LANES))
    scal[2] = jnp.broadcast_to(alpha + second * beta, (shots, LANES))

    scaled = DAMPING * mask

    def store(s):
        return pltpu.make_async_copy(wave_ref.at[:, s], wave_out.at[:, s], store_s.at[s])

    def finish(s, carry):
        numer, denom = carry
        on_rest = scal[1, pl.ds(s, 1), :]
        on_field = scal[2, pl.ds(s, 1), :]
        here = jnp.where(far(s) == 0, 1.0, 0.0)
        u_r = on_field * field[s, 0] + on_rest * rest[s, 0]
        u_i = on_field * field[s, 1] + on_rest * rest[s, 1]
        wave_ref[0, s] = u_r
        wave_ref[1, s] = u_i
        store(s).start()
        mis_r = on_field * image[s, 0] + on_rest * rest_image[s, 0] - amp_ref[0, s] * here
        mis_i = on_field * image[s, 1] + on_rest * rest_image[s, 1] - amp_ref[1, s] * here
        grad_r = -K_SQ * (u_r - scaled * u_i)
        grad_i = -K_SQ * (u_i + scaled * u_r)
        return (
            numer + grad_r * mis_r + grad_i * mis_i,
            denom + grad_r * grad_r + grad_i * grad_i,
        )

    empty = jnp.zeros((cells, width), F32)
    numer, denom = lax.fori_loop(0, shots, finish, (empty, empty))
    upd_ref[...] = slow_ref[...] - numer / (denom + REGULAR)

    def drain(s):
        sent_edges(0, field, s)
        sent_edges(1, image, s)
        sent_edges(2, normal, s)
        store(s).wait()

    each_shot(drain)

    def drain_small(k):
        routed(k).wait_send()
        shared(0, note_a, all_a, k).wait_send()
        shared(1, note_b, all_b, k).wait_send()

    others(drain_small)


def local(slowness, absorbing, src_cell, src_amp, rec_slab, rec_local, rec_data):
    count = lax.axis_size("slab")
    depth, height, width = slowness.shape
    cells = depth * height
    shots, block = rec_local.shape
    capacity = 3 * block // count
    slots = -(-capacity // LANES) * LANES
    group = min(count, SPAN // capacity)
    vmem = pl.BlockSpec(memory_space=pltpu.VMEM)
    hbm = pl.BlockSpec(memory_space=pltpu.HBM)
    smem = pl.BlockSpec(memory_space=pltpu.SMEM)
    pair = pltpu.VMEM((shots, 2, cells, width), F32)
    dma = pltpu.SemaphoreType.DMA
    wavefield, updated = pl.pallas_call(
        functools.partial(kernel, count, depth, height, slots, capacity),
        out_shape=(
            jax.ShapeDtypeStruct((2, shots, cells, width), F32),
            jax.ShapeDtypeStruct((cells, width), F32),
        ),
        in_specs=[hbm, hbm, smem, smem, hbm, hbm, hbm],
        out_specs=(hbm, vmem),
        scratch_shapes=[
            pltpu.VMEM((2, shots, cells, width), F32),
            pltpu.VMEM((cells, width), F32),
            pltpu.VMEM((cells, width), jnp.int32),
            pltpu.VMEM((shots, 1, block), jnp.int32),
            pltpu.VMEM((shots, block), jnp.int32),
            pltpu.VMEM((2, shots, block), F32),
            pltpu.VMEM((shots, 5 * cells // 2, 2 * width), F32),
            pltpu.VMEM((shots, 2 * KINDS, block), F32),
            pltpu.VMEM((shots, block), F32),
            pltpu.VMEM((count, KINDS, shots, slots), F32),
            pltpu.VMEM((count, KINDS, shots, slots), F32),
            pltpu.VMEM((count // group, 6, shots, group * capacity), F32),
            pltpu.VMEM((shots, cells, width), F32),
            pair, pair, pair, pair, pair,
            pltpu.VMEM((3, 2, shots, 2, height, width), F32),
            pltpu.VMEM((2, shots, LANES), F32),
            pltpu.VMEM((1, LANES), F32),
            pltpu.VMEM((count, 1, LANES), F32),
            pltpu.VMEM((3, shots, LANES), F32),
            pltpu.VMEM((1, LANES), F32),
            pltpu.VMEM((count, 1, LANES), F32),
            pltpu.VMEM((3, shots, LANES), F32),
            dma((5,)), dma((shots,)), dma((count,)), dma((count,)),
            dma((2, count)), dma((2, count)),
            dma((3, 2, shots)), dma((3, 2, shots)),
        ],
        compiler_params=pltpu.CompilerParams(
            collective_id=0, has_side_effects=True, vmem_limit_bytes=60 * 1024 * 1024
        ),
    )(
        slowness.reshape(cells, width),
        absorbing.reshape(cells, width),
        src_cell,
        src_amp,
        rec_slab.reshape(shots, 1, block),
        rec_local,
        rec_data,
    )
    return (
        wavefield.reshape(2, shots, depth, height, width),
        updated.reshape(depth, height, width),
    )


def solution(mesh):
    return jax.shard_map(
        local,
        mesh=mesh,
        in_specs=(
            P("slab", "groups", None),
            P("slab", "groups", None),
            P("groups"),
            P(None, "groups"),
            P("groups", "slab", None),
            P("groups", "slab"),
            P(None, "groups", "slab"),
        ),
        out_specs=(P(None, "groups", "slab", None, None), P("slab", "groups", None)),
        check_vma=False,
    )
```

```python
import functools

import jax
import jax.numpy as jnp
from jax import lax
from jax.experimental import pallas as pl
from jax.experimental.pallas import tpu as pltpu
from jax.sharding import PartitionSpec as P

K_SQ = 0.8
DAMPING = 0.6
PENALTY = 4.0
REGULAR = 0.5

LANES = 128
SPAN = 768
KINDS = 3
F32 = jnp.float32
BF16 = jnp.bfloat16
MESH = pl.DeviceIdType.MESH
NT = (((1,), (1,)), ((), ()))


def spread(row, rows):
    tile = jnp.broadcast_to(row, (16, row.shape[1])).astype(BF16)
    return jnp.concatenate([tile] * (rows // 16), axis=0)


def ramp(shape):
    return lax.broadcasted_iota(jnp.int32, shape, 0).astype(F32).astype(BF16)


def split(values):
    high = values.astype(BF16).astype(F32)
    return high, (values - high).astype(BF16).astype(F32)


def kernel(
    count, depth, height, slots, capacity,
    slow_in, absorb_in, cell_ref, amp_ref, own_in, loc_in, dat_in,
    wave_out, upd_ref,
    wave_ref, slow_ref, absorb_ref, own_ref, loc_ref, dat_ref, sums,
    feats, ranks, send, recv, parts, weight, field, image, normal, rest, rest_image,
    shell, cover, cover_in, halo, stat_a, note_a, all_a, stat_b, note_b, all_b, scal,
    load_s, store_s, route_s, route_r, sum_s, sum_r, halo_s, halo_r, cover_s, cover_r,
):
    me = lax.axis_index("slab")
    shots, block = loc_ref.shape
    cells, width = slow_ref.shape
    dot = functools.partial(lax.dot_general, preferred_element_type=F32)

    def others(body):
        lax.fori_loop(1, count, lambda k, c: (body(k), c)[1], 0)

    def each_shot(body):
        lax.fori_loop(0, shots, lambda s, c: (body(s), c)[1], 0)

    barrier = pltpu.get_barrier_semaphore()

    def greet(k):
        pl.semaphore_signal(
            barrier, inc=1, device_id={"slab": lax.rem(me + k, count)}, device_id_type=MESH
        )

    loads = [
        pltpu.make_async_copy(source, target, load_s.at[at])
        for at, (source, target) in enumerate(
            [(own_in, own_ref), (loc_in, loc_ref), (dat_in, dat_ref),
             (slow_in, slow_ref), (absorb_in, absorb_ref)]
        )
    ]
    for load in loads:
        load.start()
    others(greet)
    for load in loads[:3]:
        load.wait()

    own, loc = own_ref[:, 0, :], loc_ref[...]
    column = loc & (width - 1)
    real_hi, real_lo = split(dat_ref[0])
    imag_hi, imag_lo = split(dat_ref[1])
    rows = [(loc - column).astype(F32), (column + 1).astype(F32)]
    rows += [real_hi, real_lo, imag_hi, imag_lo]
    for at, row in enumerate(rows):
        feats[:, at, :] = row
    named = jnp.concatenate(
        [jnp.where(own == slab, 1.0, 0.0) for slab in range(count)], axis=0
    )
    first = lax.broadcasted_iota(jnp.int32, (block, block), 0)
    later = lax.broadcasted_iota(jnp.int32, (block, block), 1)
    before = jnp.where(first < later, 1.0, 0.0).astype(BF16)
    ahead = dot(named.astype(BF16), before, (((1,), (0,)), ((), ())))
    chosen = named * ahead
    rank = chosen[:shots]
    for slab in range(1, count):
        rank = rank + chosen[slab * shots : (slab + 1) * shots]
    ranks[...] = rank

    slot = ramp((slots, block))
    slab_of = ramp((count, block))
    one = jnp.ones((), BF16)
    nought = jnp.zeros((), BF16)

    def compact(s):
        right = jnp.where(slot == spread(ranks[pl.ds(s, 1), :], slots), one, nought)
        mine = slab_of == spread(own_ref[s].astype(F32), count)
        left = jnp.concatenate(
            [
                jnp.where(mine, spread(feats[s, at : at + 1, :], count), nought)
                for at in range(2 * KINDS)
            ],
            axis=0,
        )
        out = dot(left, right, NT)
        for kind in range(KINDS):
            at = 2 * kind * count
            value = out[at : at + count] + out[at + count : at + 2 * count]
            send[:, kind, pl.ds(s, 1), :] = value.reshape(count, 1, slots)

    each_shot(compact)
    pl.semaphore_wait(barrier, count - 1)

    def routed(k):
        target = lax.rem(me + k, count)
        return pltpu.make_async_remote_copy(
            src_ref=send.at[target], dst_ref=recv.at[k],
            send_sem=route_s.at[k], recv_sem=route_r.at[k],
            device_id={"slab": target}, device_id_type=MESH,
        )

    others(lambda k: routed(k).start())
    recv[0] = send[me]
    for load in loads[3:]:
        load.wait()

    coeff = K_SQ * slow_ref[...]
    mask = absorb_ref[...].astype(F32)
    lossy = DAMPING * coeff * mask
    row_of = lax.broadcasted_iota(jnp.int32, (cells, width), 0)
    x_of = lax.broadcasted_iota(jnp.int32, (cells, width), 1)
    z_of = row_of // height + me * depth
    y_of = row_of % height
    at_top, at_bottom = y_of == 0, y_of == height - 1
    at_left, at_right = x_of == 0, x_of == width - 1

    def far(s):
        cell = cell_ref[s]
        plane = cell // (height * width)
        line = (cell // width) % height
        place = cell % width
        return jnp.abs(z_of - plane) + jnp.abs(y_of - line) + jnp.abs(x_of - place)

    def laplace(centre, low, high):
        rows = centre.shape[0]
        beside = jnp.concatenate([centre[height:], high] if rows > height else [high], axis=0)
        beside = beside + jnp.concatenate([low, centre[:-height]] if rows > height else [low], axis=0)
        beside = beside + jnp.where(at_top[:rows], 0.0, pltpu.roll(centre, 1, 0))
        beside = beside + jnp.where(at_bottom[:rows], 0.0, pltpu.roll(centre, rows - 1, 0))
        beside = beside + jnp.where(at_left[:rows], 0.0, pltpu.roll(centre, 1, 1))
        beside = beside + jnp.where(at_right[:rows], 0.0, pltpu.roll(centre, width - 1, 1))
        return 6.0 * centre - beside

    def helmholtz(real, imag, low, high, sign, cover=None):
        size, loss = (coeff, lossy) if cover is None else cover
        out_r = laplace(real, low[0], high[0]) - size * real + sign * loss * imag
        out_i = laplace(imag, low[1], high[1]) - size * imag - sign * loss * real
        return out_r, out_i

    for side, last in enumerate((0, count - 1)):
        @pl.when(me == last)
        def _(side=side):
            shell[side] = jnp.zeros(shell.shape[1:], F32)
            halo[1, side] = jnp.zeros(halo.shape[2:], F32)
            cover_in[side] = jnp.zeros(cover_in.shape[1:], F32)

    for side, at in enumerate((cells - height, 0)):
        cover[side, 0] = coeff[at : at + height]
        cover[side, 1] = lossy[at : at + height]

    def edge(step, ref, s, side):
        target = me + 1 if side == 0 else me - 1
        deep = 2 * height if step == 0 else height
        at = cells - deep if side == 0 else 0
        landing = shell.at[side, s] if step == 0 else halo.at[step - 1, side, s]
        return pltpu.make_async_remote_copy(
            src_ref=ref.at[s, :, pl.ds(at, deep), :], dst_ref=landing,
            send_sem=halo_s.at[step, side, s], recv_sem=halo_r.at[step, side, s],
            device_id={"slab": target}, device_id_type=MESH,
        )

    has = [me > 0, me < count - 1]

    def cover_edge(side):
        return pltpu.make_async_remote_copy(
            src_ref=cover.at[side], dst_ref=cover_in.at[side],
            send_sem=cover_s.at[side], recv_sem=cover_r.at[side],
            device_id={"slab": me + 1 if side == 0 else me - 1}, device_id_type=MESH,
        )

    pl.when(has[1])(lambda: cover_edge(0).start())
    pl.when(has[0])(lambda: cover_edge(1).start())

    def send_edges(step, ref, s):
        pl.when(has[1])(lambda: edge(step, ref, s, 0).start())
        pl.when(has[0])(lambda: edge(step, ref, s, 1).start())

    def wait_edges(step, ref, s):
        pl.when(has[0])(lambda: edge(step, ref, s, 0).wait_recv())
        pl.when(has[1])(lambda: edge(step, ref, s, 1).wait_recv())

    def sent_edges(step, ref, s):
        pl.when(has[1])(lambda: edge(step, ref, s, 0).wait_send())
        pl.when(has[0])(lambda: edge(step, ref, s, 1).wait_send())

    def along(values):
        return jnp.sum(values, axis=0, keepdims=True)

    def shared(which, note, gathered, k):
        return pltpu.make_async_remote_copy(
            src_ref=note, dst_ref=gathered.at[k],
            send_sem=sum_s.at[which, k], recv_sem=sum_r.at[which, k],
            device_id={"slab": lax.rem(me + k, count)}, device_id_type=MESH,
        )

    def diagonal(values):
        lane = lax.broadcasted_iota(jnp.int32, values.shape, 1)
        return jnp.where(lane == lax.broadcasted_iota(jnp.int32, values.shape, 0), values, 0.0)

    def share(which, stat, note, gathered):
        kinds = stat.shape[0] * shots
        own_sums = jnp.sum(stat[...].reshape(kinds, LANES), axis=1, keepdims=True)
        note[...] = along(diagonal(jnp.broadcast_to(own_sums, (kinds, LANES))))
        others(lambda k: shared(which, note, gathered, k).start())
        gathered[0] = note[...]

    def totals(which, stat, note, gathered):
        others(lambda k: shared(which, note, gathered, k).wait_recv())
        kinds = stat.shape[0] * shots
        line = jnp.sum(gathered[...], axis=0)
        column = jnp.sum(
            diagonal(jnp.broadcast_to(line, (kinds, LANES))), axis=1, keepdims=True
        )
        return [column[at : at + shots] for at in range(0, kinds, shots)]

    group = min(count, SPAN // capacity)
    wide = group * capacity
    half = cells // 2
    cell_row = ramp((half, wide))
    cell_col = ramp((2 * width, wide))

    def gather(base, s):
        def line(kind, length):
            return spread(parts[base // group, kind, pl.ds(s, 1), :], length)

        right = jnp.where(cell_col == line(1, 2 * width), one, nought)
        same = cell_row == line(0, half)
        left = jnp.concatenate(
            [jnp.where(same, one, nought)]
            + [jnp.where(same, line(kind, half), nought) for kind in range(2, 6)],
            axis=0,
        )
        total = dot(left, right, NT)
        if base > 0:
            total = sums[s] + total
        if base + group < count:
            sums[s] = total
            return

        def field_of(at):
            piece = total[at * half : (at + 1) * half]
            return jnp.concatenate([piece[:, :width], piece[:, width:]], axis=0)

        weight[s] = PENALTY * field_of(0)
        data_r = field_of(1) + field_of(2)
        data_i = field_of(3) + field_of(4)
        away = far(s)
        here = jnp.where(away == 0, 1.0, 0.0)
        lap = jnp.where(away == 0, 6.0, jnp.where(away == 1, -1.0, 0.0)) - coeff * here
        turn = lossy * here
        amp_r, amp_i = amp_ref[0, s], amp_ref[1, s]
        field[s, 0] = amp_r * lap - amp_i * turn + PENALTY * data_r
        field[s, 1] = amp_i * lap + amp_r * turn + PENALTY * data_i
        send_edges(0, field, s)

    for base in range(0, count, group):
        for k in range(max(base, 1), base + group):
            routed(k).wait_recv()
        cell, real, imag = [
            jnp.concatenate(
                [recv[k, kind][:, :capacity] for k in range(base, base + group)], axis=1
            )
            for kind in range(KINDS)
        ]
        cell = cell.astype(jnp.int32) - 1
        line_of = cell >> (width.bit_length() - 1)
        place = (cell & (width - 1)) + jnp.where(line_of >= half, width, 0)
        at = base // group
        parts[at, 0] = (line_of & (half - 1)).astype(F32)
        parts[at, 1] = jnp.where(cell < 0, -1, place).astype(F32)
        parts[at, 2], parts[at, 3] = split(real)
        parts[at, 4], parts[at, 5] = split(imag)
        each_shot(functools.partial(gather, base))

    pl.when(has[0])(lambda: cover_edge(0).wait_recv())
    pl.when(has[1])(lambda: cover_edge(1).wait_recv())

    def apply_first(s):
        wait_edges(0, field, s)
        r, i = field[s, 0], field[s, 1]
        low, high = shell[0, s], shell[1, s]
        out_r, out_i = helmholtz(r, i, low[:, height:], high[:, :height], 1.0)
        image[s, 0] = out_r
        image[s, 1] = out_i
        before_r, before_i = helmholtz(
            low[0, height:], low[1, height:], low[:, :height],
            (r[:height], i[:height]), 1.0, (cover_in[0, 0], cover_in[0, 1]),
        )
        after_r, after_i = helmholtz(
            high[0, :height], high[1, :height], (r[-height:], i[-height:]),
            high[:, height:], 1.0, (cover_in[1, 0], cover_in[1, 1]),
        )
        inner_low = jnp.where(me > 0, 1.0, 0.0)
        inner_high = jnp.where(me < count - 1, 1.0, 0.0)
        halo[0, 0, s, 0] = inner_low * before_r
        halo[0, 0, s, 1] = inner_low * before_i
        halo[0, 1, s, 0] = inner_high * after_r
        halo[0, 1, s, 1] = inner_high * after_i
        size = r * r + i * i
        stat_a[0, pl.ds(s, 1), :] = along(size)
        stat_a[1, pl.ds(s, 1), :] = along(out_r * out_r + out_i * out_i + weight[s] * size)

    each_shot(apply_first)
    share(0, stat_a, note_a, all_a)

    def apply_back(s):
        out_r, out_i = helmholtz(image[s, 0], image[s, 1], halo[0, 0, s], halo[0, 1, s], -1.0)
        normal[s, 0] = out_r + weight[s] * field[s, 0]
        normal[s, 1] = out_i + weight[s] * field[s, 1]
        send_edges(2, normal, s)

    each_shot(apply_back)
    norm, curve = totals(0, stat_a, note_a, all_a)
    alpha = norm / curve
    scal[0] = jnp.broadcast_to(alpha, (shots, LANES))

    def apply_second(s):
        wait_edges(2, normal, s)
        step = scal[0, pl.ds(s, 1), :]
        r = field[s, 0] - step * normal[s, 0]
        i = field[s, 1] - step * normal[s, 1]
        low = shell[0, s][:, height:] - step[None] * halo[1, 0, s]
        high = shell[1, s][:, :height] - step[None] * halo[1, 1, s]
        out_r, out_i = helmholtz(r, i, low, high, 1.0)
        rest[s, 0] = r
        rest[s, 1] = i
        rest_image[s, 0] = out_r
        rest_image[s, 1] = out_i
        size = r * r + i * i
        stat_b[0, pl.ds(s, 1), :] = along(size)
        stat_b[1, pl.ds(s, 1), :] = along(out_r * out_r + out_i * out_i + weight[s] * size)
        stat_b[2, pl.ds(s, 1), :] = along(
            out_r * image[s, 0] + out_i * image[s, 1]
            + weight[s] * (r * field[s, 0] + i * field[s, 1])
        )

    each_shot(apply_second)
    share(1, stat_b, note_b, all_b)
    following, own_curve, cross = totals(1, stat_b, note_b, all_b)
    beta = following / norm
    second = following / (own_curve + beta * (2.0 * cross + beta * curve))
    scal[1] = jnp.broadcast_to(second, (shots, LANES))
    scal[2] = jnp.broadcast_to(alpha + second * beta, (shots, LANES))

    scaled = DAMPING * mask

    def store(s):
        return pltpu.make_async_copy(wave_ref.at[:, s], wave_out.at[:, s], store_s.at[s])

    def finish(s, carry):
        numer, denom = carry
        on_rest = scal[1, pl.ds(s, 1), :]
        on_field = scal[2, pl.ds(s, 1), :]
        here = jnp.where(far(s) == 0, 1.0, 0.0)
        u_r = on_field * field[s, 0] + on_rest * rest[s, 0]
        u_i = on_field * field[s, 1] + on_rest * rest[s, 1]
        wave_ref[0, s] = u_r
        wave_ref[1, s] = u_i
        store(s).start()
        mis_r = on_field * image[s, 0] + on_rest * rest_image[s, 0] - amp_ref[0, s] * here
        mis_i = on_field * image[s, 1] + on_rest * rest_image[s, 1] - amp_ref[1, s] * here
        grad_r = -K_SQ * (u_r - scaled * u_i)
        grad_i = -K_SQ * (u_i + scaled * u_r)
        return (
            numer + grad_r * mis_r + grad_i * mis_i,
            denom + grad_r * grad_r + grad_i * grad_i,
        )

    empty = jnp.zeros((cells, width), F32)
    numer, denom = lax.fori_loop(0, shots, finish, (empty, empty))
    upd_ref[...] = slow_ref[...] - numer / (denom + REGULAR)

    def drain(s):
        sent_edges(0, field, s)
        sent_edges(2, normal, s)
        store(s).wait()

    pl.when(has[1])(lambda: cover_edge(0).wait_send())
    pl.when(has[0])(lambda: cover_edge(1).wait_send())
    each_shot(drain)

    def drain_small(k):
        routed(k).wait_send()
        shared(0, note_a, all_a, k).wait_send()
        shared(1, note_b, all_b, k).wait_send()

    others(drain_small)


def local(slowness, absorbing, src_cell, src_amp, rec_slab, rec_local, rec_data):
    count = lax.axis_size("slab")
    depth, height, width = slowness.shape
    cells = depth * height
    shots, block = rec_local.shape
    capacity = 3 * block // count
    slots = -(-capacity // LANES) * LANES
    group = min(count, SPAN // capacity)
    vmem = pl.BlockSpec(memory_space=pltpu.VMEM)
    hbm = pl.BlockSpec(memory_space=pltpu.HBM)
    smem = pl.BlockSpec(memory_space=pltpu.SMEM)
    pair = pltpu.VMEM((shots, 2, cells, width), F32)
    dma = pltpu.SemaphoreType.DMA
    wavefield, updated = pl.pallas_call(
        functools.partial(kernel, count, depth, height, slots, capacity),
        out_shape=(
            jax.ShapeDtypeStruct((2, shots, cells, width), F32),
            jax.ShapeDtypeStruct((cells, width), F32),
        ),
        in_specs=[hbm, hbm, smem, smem, hbm, hbm, hbm],
        out_specs=(hbm, vmem),
        scratch_shapes=[
            pltpu.VMEM((2, shots, cells, width), F32),
            pltpu.VMEM((cells, width), F32),
            pltpu.VMEM((cells, width), jnp.int32),
            pltpu.VMEM((shots, 1, block), jnp.int32),
            pltpu.VMEM((shots, block), jnp.int32),
            pltpu.VMEM((2, shots, block), F32),
            pltpu.VMEM((shots, 5 * cells // 2, 2 * width), F32),
            pltpu.VMEM((shots, 2 * KINDS, block), F32),
            pltpu.VMEM((shots, block), F32),
            pltpu.VMEM((count, KINDS, shots, slots), F32),
            pltpu.VMEM((count, KINDS, shots, slots), F32),
            pltpu.VMEM((count // group, 6, shots, group * capacity), F32),
            pltpu.VMEM((shots, cells, width), F32),
            pair, pair, pair, pair, pair,
            pltpu.VMEM((2, shots, 2, 2 * height, width), F32),
            pltpu.VMEM((2, 2, height, width), F32),
            pltpu.VMEM((2, 2, height, width), F32),
            pltpu.VMEM((2, 2, shots, 2, height, width), F32),
            pltpu.VMEM((2, shots, LANES), F32),
            pltpu.VMEM((1, LANES), F32),
            pltpu.VMEM((count, 1, LANES), F32),
            pltpu.VMEM((3, shots, LANES), F32),
            pltpu.VMEM((1, LANES), F32),
            pltpu.VMEM((count, 1, LANES), F32),
            pltpu.VMEM((3, shots, LANES), F32),
            dma((5,)), dma((shots,)), dma((count,)), dma((count,)),
            dma((2, count)), dma((2, count)),
            dma((3, 2, shots)), dma((3, 2, shots)), dma((2,)), dma((2,)),
        ],
        compiler_params=pltpu.CompilerParams(
            collective_id=0, has_side_effects=True, vmem_limit_bytes=60 * 1024 * 1024
        ),
    )(
        slowness.reshape(cells, width),
        absorbing.reshape(cells, width),
        src_cell,
        src_amp,
        rec_slab.reshape(shots, 1, block),
        rec_local,
        rec_data,
    )
    return (
        wavefield.reshape(2, shots, depth, height, width),
        updated.reshape(depth, height, width),
    )


def solution(mesh):
    return jax.shard_map(
        local,
        mesh=mesh,
        in_specs=(
            P("slab", "groups", None),
            P("slab", "groups", None),
            P("groups"),
            P(None, "groups"),
            P("groups", "slab", None),
            P("groups", "slab"),
            P(None, "groups", "slab"),
        ),
        out_specs=(P(None, "groups", "slab", None, None), P("slab", "groups", None)),
        check_vma=False,
    )
```
